32 devices in a mesh: lat: 8 (over y, x, core), lon: 4 (over z).
Axes of the slice: x: 2, y: 2, z: 4, core: 2. Of those that a mesh axis runs over, the one named last changes fastest.
Arguments:
- gaussian_thermal_state: float32 [16, 1280, 2560], P(None, 'lat', 'lon'), may hold values from -6 to 6
- radiation_holder_device: int32 [32, 25600, 1], P(('lat', 'lon')), may hold values from 0 to 31; in each aligned block of 25600 rows (0 to 25599, 25600 to 51199, ..., all dimensions but the last counted through in order) at most 1280 rows name the same one
- layer_opacity_depths: bfloat16 [32, 16, 16, 40960], P(('lat', 'lon')), may hold values from 0.049804688 to 3
- wavenumber_duos_placed: int32 [640], replicated, may hold values from 0 to 639, each once
- reduced_grid_sites: int32 [1280], P('lat'), may hold values from 640 to 2560
- weighted_polynomial_basis: bfloat16 [640, 1280, 1344], P(('lat', 'lon')), may hold values from -0.15625 to 0.15625
Outputs:
- new_temperature: float32 [16, 1280, 2560], P(None, 'lat', 'lon')
The draws below stay inside these ranges and needn't reach their ends.
Inputs may be any that keep to these rules, and one draw needn't show every extreme that they name: `radiation_holder_device`: in each block d no owner is named by more than 1280 of the block's 25600 columns; some owner is named by exactly 1280 in some blocks. `wavenumber_duos_placed`: each pair number appears in exactly one slot.
All inputs are finite; a program needn't handle non-finite values.
Results may differ from the reference program's by a relative error of at most 0.0072.
Values may be sent and summed in bfloat16 or wider, within the bound.
A program may use at most 448 MiB of HBM per device.

```python
import math
import jax
import jax.numpy as jnp
import numpy as np
from jax import lax

GAUSS_PARALLELS = 1280
MERIDIAN_TOTAL = 2560
BANDS = 16
NDEG = 1344
VERTICAL_LAYERS = 16
NWAVE = 1280
PAIRS = 640
CLAT = 80
CLON = 320
COLS_DEV = 25600
CAP = 1280
N_LAT = 8
N_LON = 4
DEVICES = 32


def place_ends(entries, key, smallest, high):
    dims = entries.shape
    place = [jax.random.randint(jax.random.fold_in(key, axis), (), 0, dims[axis]) for axis in range(len(dims))]
    entries = entries.at[tuple(place)].set(smallest)
    longest = dims.index(max(dims))
    place[longest] = (place[longest] + 1) % dims[longest]
    return entries.at[tuple(place)].set(high)


def levels(rng, shape, cuts, least, high):
    level, own = 1.0, jax.random.fold_in(rng, 6)
    for dim, blocks in cuts:
        heights = jnp.exp(jax.random.uniform(jax.random.fold_in(own, dim), (blocks,), jnp.float32, least / len(cuts), high / len(cuts)))
        level = level * jnp.repeat(heights, shape[dim] // blocks).reshape([-1 if axis == dim else 1 for axis in range(len(shape))])
    return level


def deal_out(rng, own, number, rows, count, top, reach, lean):
    ranking = jax.random.permutation(rng, count)
    crowded, usual = portions_of(count, rows * top, reach, lean, True), portions_of(count, rows * top, reach, lean, False)
    places = jnp.arange(count)

    def named(sizes, turn):
        used = int((sizes > 0).sum())
        fixed = max(1, used // 4)
        moved = fixed + (places - fixed + turn * (used - fixed)) % max(1, count - fixed)
        return jnp.zeros((count,), jnp.int32).at[ranking[jnp.where(places < fixed, places, moved)]].set(jnp.asarray(sizes, jnp.int32))

    sizes = jnp.where(number % 4 == 0, named(crowded, number // 4), named(usual, number - number // 4 - 1))
    mixed = jax.random.permutation(jax.random.fold_in(own, 3), count)
    donor, taker = mixed[0:count // 2 * 2:2], mixed[1:count // 2 * 2:2]
    room = jnp.minimum(sizes[donor] - 1, reach - sizes[taker]) // 2
    room = jnp.where((donor == ranking[0]) | (taker == ranking[0]) | (sizes[taker] == 0), 0, jnp.maximum(room, 0))
    moved = jax.random.randint(jax.random.fold_in(own, 4), (count // 2,), 0, 1 << 20) % (room + 1)
    sizes = sizes.at[donor].add(-moved).at[taker].add(moved)
    items = jnp.searchsorted(jnp.cumsum(sizes), jnp.arange(rows * top), side="right").astype(jnp.int32)
    grid = items.reshape(top, rows).T
    grid = grid[jax.random.permutation(jax.random.fold_in(own, 1), rows)]
    turn = jax.random.randint(jax.random.fold_in(own, 2), (rows, 1), 0, top)
    return jnp.take_along_axis(grid, (jnp.arange(top)[None, :] + turn) % top, axis=1)


def portions_of(number_of, total, bound, lean, full):
    loads = [(1 << 20) // math.isqrt(standing ** lean) + 1 for standing in range(1, number_of + 1)]
    largest = bound if full else min(bound, max(-(-total // number_of), total * loads[0] // sum(loads)))
    least = 1 if total - largest >= number_of - 1 else 0
    holding, rest = [largest] + [least] * (number_of - 1), total - largest - least * (number_of - 1)
    while rest > 0:
        movable = [i for i in range(1, number_of) if holding[i] < largest] or [i for i in range(1, number_of) if holding[i] < bound]
        mass, budget = sum([loads[i] for i in movable]), rest
        for i in movable:
            addition = min(bound - holding[i], max(1, budget * loads[i] // mass), rest)
            holding[i] = holding[i] + addition
            rest = rest - addition
    return np.array(holding)


def scatter_about(key, extent, spread, most, cuts=(), kind=jnp.bfloat16):
    level = levels(key, extent, cuts, -0.22, 0.18) if cuts else 1.0
    values = jax.random.normal(key, extent, jnp.float32) * spread * level
    return jnp.minimum(jnp.maximum(values, -most), most).astype(kind)


def setup_inputs(seed: int = 0) -> dict:
    keys = jax.random.split(jax.random.key(seed), 7)
    gaussian_thermal_state = scatter_about(keys[0], (VERTICAL_LAYERS, GAUSS_PARALLELS, MERIDIAN_TOTAL), 1.0, 6.0, ((1, 8), (2, 4)), jnp.float32)
    radiation_holder_device_keys = jax.random.split(jax.random.fold_in(keys[1], 1), DEVICES * COLS_DEV // COLS_DEV)
    radiation_holder_device_turns = jax.random.permutation(jax.random.fold_in(keys[1], 3), DEVICES * COLS_DEV // COLS_DEV)
    radiation_holder_device = jax.vmap(lambda own, number: deal_out(jax.random.fold_in(keys[1], 2), own, number, COLS_DEV, DEVICES, 1, CAP, 2))(radiation_holder_device_keys, radiation_holder_device_turns).reshape((DEVICES, COLS_DEV, 1))
    layer_opacity_depths = jnp.clip(jnp.exp(math.log(3.0) - 4.0982585 * jax.random.uniform(keys[2], (DEVICES, VERTICAL_LAYERS, BANDS, DEVICES * CAP), jnp.float32) ** levels(keys[2], (DEVICES, VERTICAL_LAYERS, BANDS, DEVICES * CAP), ((0, 32),), -0.2, 0.2)), 0.049804688, 3.0).astype(jnp.bfloat16)
    wavenumber_duos_placed = jax.random.permutation(keys[3], PAIRS).astype(jnp.int32)
    reduced_grid_sites = place_ends(jax.random.randint(keys[4], (GAUSS_PARALLELS,), MERIDIAN_TOTAL // 4, MERIDIAN_TOTAL + 1), jax.random.fold_in(keys[4], 1), MERIDIAN_TOTAL // 4, MERIDIAN_TOTAL).astype(jnp.int32)
    weighted_polynomial_basis = scatter_about(keys[5], (PAIRS, GAUSS_PARALLELS, NDEG), GAUSS_PARALLELS ** -0.5, 0.15625, ((0, 32),))
    return dict(gaussian_thermal_state=gaussian_thermal_state, radiation_holder_device=radiation_holder_device, layer_opacity_depths=layer_opacity_depths, wavenumber_duos_placed=wavenumber_duos_placed, reduced_grid_sites=reduced_grid_sites, weighted_polynomial_basis=weighted_polynomial_basis)


DIFFUSION = 4.0

def wave_numbers(pairs, nwave):
    repeated = jnp.repeat(pairs, 4)
    which = jnp.tile(jnp.array([0, 0, 1, 1], dtype=jnp.int32), pairs.shape[0])
    return jnp.where(which == 0, repeated, nwave - 1 - repeated)

def dft_table(waves, nlon):
    places = jnp.arange(nlon, dtype=jnp.int32)
    phase = places[:, None] * waves[None, :] % nlon
    angle = phase.astype(jnp.float32) * (2.0 * math.pi / nlon)
    parity = jnp.arange(waves.shape[0], dtype=jnp.int32) % 2
    values = jnp.where(parity[None, :] == 0, jnp.cos(angle), jnp.sin(angle))
    return (values * (1.0 / math.sqrt(nlon))).astype(jnp.bfloat16)

def owner_ranks(owner, devices_all):
    matches = (owner[:, None] == jnp.arange(devices_all, dtype=jnp.int32)[None, :]).astype(jnp.int32)
    counts = lax.optimization_barrier(jnp.sum(matches, axis=0))
    starts = jnp.cumsum(counts) - counts
    start_each = lax.optimization_barrier(jnp.sum(matches * starts[None, :], axis=1))
    order = jnp.argsort(owner, stable=True)
    position = jnp.zeros_like(owner).at[order].set(jnp.arange(owner.shape[0], dtype=jnp.int32))
    return position - start_each

def flux_step(flux, inputs):
    passing, planck = inputs
    fresh = passing * flux + (1.0 - passing) * planck
    return (fresh, fresh)

def radiate(column_temp, depth):
    bands = depth.shape[1]
    source = jnp.exp(0.5 * column_temp.astype(jnp.float32))
    weights = (jnp.arange(bands, dtype=jnp.float32) + 1.0) * (2.0 / (bands * (bands + 1)))
    passing = jnp.exp(-depth.astype(jnp.float32))
    planck = weights[None, :, None] * source[:, None, :]
    _, below = lax.scan(flux_step, jnp.zeros_like(planck[0]), (passing, planck))
    above = jnp.concatenate([jnp.zeros_like(planck[:1]), below[:-1]], axis=0)
    _, upper = lax.scan(flux_step, planck[-1], (passing, planck), reverse=True)
    under = jnp.concatenate([upper[1:], planck[-1:]], axis=0)
    return lax.optimization_barrier(jnp.sum(above - below + under - upper, axis=1))

def reference(gaussian_thermal_state, radiation_holder_device, layer_opacity_depths, wavenumber_duos_placed, reduced_grid_sites, weighted_polynomial_basis):
    vertical_layer_pile = gaussian_thermal_state.shape[0]
    nwave = NWAVE
    reduced_resolution_grid = (gaussian_thermal_state[:, 0::2, 0::2] + gaussian_thermal_state[:, 1::2, 0::2] + (gaussian_thermal_state[:, 0::2, 1::2] + gaussian_thermal_state[:, 1::2, 1::2])) * 0.25
    reduced_resolution_grid = reduced_resolution_grid.astype(jnp.bfloat16)
    blocks = reduced_resolution_grid.reshape(vertical_layer_pile, N_LAT, CLAT, N_LON, CLON).transpose(1, 3, 0, 2, 4).reshape(DEVICES, vertical_layer_pile, CLAT * CLON)

    def block_heat(inputs):
        block_temp, block_owner, block_index = inputs
        owner = block_owner[:, 0]
        slots = block_index * CAP + owner_ranks(owner, DEVICES)
        depth = jnp.transpose(layer_opacity_depths[owner, :, :, slots], (1, 2, 0))
        return radiate(block_temp, depth).astype(jnp.bfloat16)
    heat_blocks = lax.map(block_heat, (blocks, radiation_holder_device, jnp.arange(DEVICES, dtype=jnp.int32)))
    coarse_heat = heat_blocks.reshape(N_LAT, N_LON, vertical_layer_pile, CLAT, CLON).transpose(2, 0, 3, 1, 4).reshape(vertical_layer_pile, GAUSS_PARALLELS // 2, MERIDIAN_TOTAL // 2)
    full_resolution_warming = jnp.repeat(jnp.repeat(coarse_heat, 2, axis=1), 2, axis=2)
    radiatively_driven_thermal = (gaussian_thermal_state + full_resolution_warming.astype(jnp.float32)).astype(jnp.bfloat16)
    waves = wave_numbers(wavenumber_duos_placed, nwave)
    table = dft_table(waves, MERIDIAN_TOTAL)
    ncol = waves.shape[0]
    fourier = jnp.dot(radiatively_driven_thermal.reshape(vertical_layer_pile * GAUSS_PARALLELS, MERIDIAN_TOTAL), table, preferred_element_type=jnp.float32).reshape(vertical_layer_pile, GAUSS_PARALLELS, ncol)
    keep = 2 * waves[None, :] < reduced_grid_sites[:, None]
    fourier = jnp.where(keep[None], fourier, 0.0).astype(jnp.bfloat16)
    right_all = fourier.reshape(vertical_layer_pile, GAUSS_PARALLELS, PAIRS, 4).transpose(2, 0, 1, 3)
    coeff = jnp.arange(NDEG, dtype=jnp.int32)

    def per_slot(inputs):
        basis, right, pair = inputs
        right = right.reshape(vertical_layer_pile, GAUSS_PARALLELS, 2, 2).transpose(1, 2, 0, 3).reshape(GAUSS_PARALLELS, 4 * vertical_layer_pile)
        full = lax.dot_general(basis, right, (((0,), (0,)), ((), ())), preferred_element_type=jnp.float32)
        full = full.reshape(NDEG, 2, 2 * vertical_layer_pile)
        first = coeff < nwave - pair
        chosen = jnp.where(first[:, None], full[:, 0], full[:, 1])
        degree = jnp.where(first, pair + coeff, coeff - 1).astype(jnp.float32)
        factor = jnp.where(coeff <= nwave, 1.0 / (1.0 + DIFFUSION * degree * (degree + 1.0) / (nwave * nwave)), 0.0)
        damped = (chosen * factor[:, None]).astype(jnp.bfloat16)
        blank = jnp.zeros_like(damped)
        split = jnp.stack([jnp.where(first[:, None], damped, blank), jnp.where(first[:, None], blank, damped)], axis=1)
        synth = jnp.dot(basis, split.reshape(NDEG, 4 * vertical_layer_pile), preferred_element_type=jnp.float32)
        return synth.astype(jnp.bfloat16)
    synth_all = lax.map(per_slot, (weighted_polynomial_basis, right_all, wavenumber_duos_placed))
    synth = synth_all.reshape(PAIRS, GAUSS_PARALLELS, 2, vertical_layer_pile, 2).transpose(3, 1, 0, 2, 4).reshape(vertical_layer_pile * GAUSS_PARALLELS, ncol)
    result = lax.dot_general(synth, table, (((1,), (1,)), ((), ())), preferred_element_type=jnp.float32)
    return result.reshape(vertical_layer_pile, GAUSS_PARALLELS, MERIDIAN_TOTAL)
```

```python
import math

import jax
import jax.numpy as jnp
from jax import lax
from jax.experimental import pallas as pl
from jax.experimental.pallas import tpu as pltpu
from jax.sharding import PartitionSpec as P

DIFFUSION = 4.0


def wave_numbers(pairs, nwave):
    repeated = jnp.repeat(pairs, 4)
    which = jnp.tile(jnp.array([0, 0, 1, 1], dtype=jnp.int32), pairs.shape[0])
    return jnp.where(which == 0, repeated, nwave - 1 - repeated)


def turn_angles(places, waves, nlon):
    phase = places[:, None] * waves[None, :] % nlon
    return phase.astype(jnp.float32) * (2.0 * math.pi / nlon)


def dft_table(waves, nlon):
    fine = 32
    while nlon % fine:
        fine //= 2
    high = turn_angles(jnp.arange(nlon // fine, dtype=jnp.int32) * fine, waves, nlon)
    low = turn_angles(jnp.arange(fine, dtype=jnp.int32), waves, nlon)
    even = (jnp.arange(waves.shape[0], dtype=jnp.int32) % 2 == 0)[None, :]
    scale = 1.0 / math.sqrt(nlon)
    cos_high, sin_high = jnp.cos(high) * scale, jnp.sin(high) * scale
    with_cos = jnp.where(even, cos_high, sin_high)
    with_sin = jnp.where(even, -sin_high, cos_high)
    with_cos, with_sin, cos_low, sin_low = lax.optimization_barrier(
        (with_cos, with_sin, jnp.cos(low), jnp.sin(low))
    )
    table = with_cos[:, None] * cos_low[None] + with_sin[:, None] * sin_low[None]
    table = table.astype(jnp.bfloat16).reshape(nlon, waves.shape[0])
    return lax.optimization_barrier(table)


def owner_ranks(owner, devices_all):
    matches = (owner[:, None] == jnp.arange(devices_all, dtype=jnp.int32)[None, :]).astype(
        jnp.int32
    )
    counts = jnp.sum(matches, axis=0)
    starts = jnp.cumsum(counts) - counts
    start_each = jnp.sum(matches * starts[None, :], axis=1)
    position = jnp.argsort(jnp.argsort(owner, stable=True))
    return position.astype(jnp.int32) - start_each


def radiate_kernel(temp_ref, depth_ref, out_ref, source_ref, heat_ref):
    layers, bands, width = depth_ref.shape
    chunk = 256 if width % 256 == 0 else 128
    source_ref[...] = jnp.exp(0.5 * temp_ref[...].astype(jnp.float32))

    def columns(i, carry):
        part = pl.ds(pl.multiple_of(i * chunk, chunk), chunk)
        band = lax.broadcasted_iota(jnp.int32, (bands, chunk), 0).astype(jnp.float32)
        weights = (band + 1.0) * (2.0 / (bands * (bands + 1)))
        taken = [
            1.0 - jnp.exp(-depth_ref[l, :, part].astype(jnp.float32)) for l in range(layers)
        ]
        planck = lambda l: weights * source_ref[l : l + 1, part]
        flux = jnp.zeros((bands, chunk), jnp.float32)
        sums = []
        for l in range(layers):
            change = taken[l] * (flux - planck(l))
            flux = flux - change
            sums.append(change)
        flux = planck(layers - 1)
        for l in reversed(range(layers)):
            change = taken[l] * (flux - planck(l))
            flux = flux - change
            heat_ref[l : l + 1, part] = jnp.sum(sums[l] + change, axis=0, keepdims=True)
        return carry

    lax.fori_loop(0, width // chunk, columns, 0)
    out_ref[...] = heat_ref[...].astype(jnp.bfloat16)


def radiate(column_temp, depth):
    layers, bands, total = depth.shape
    width = 2048
    while total % width:
        width //= 2
    return pl.pallas_call(
        radiate_kernel,
        grid=(total // width,),
        out_shape=jax.ShapeDtypeStruct((layers, total), jnp.bfloat16),
        in_specs=[
            pl.BlockSpec((layers, width), lambda i: (0, i)),
            pl.BlockSpec((layers, bands, width), lambda i: (0, 0, i)),
        ],
        out_specs=pl.BlockSpec((layers, width), lambda i: (0, i)),
        scratch_shapes=[pltpu.VMEM((layers, width), jnp.float32)] * 2,
        compiler_params=pltpu.CompilerParams(vmem_limit_bytes=24 << 20),
        cost_estimate=pl.CostEstimate(
            flops=12 * layers * bands * total,
            bytes_accessed=2 * layers * bands * total,
            transcendentals=layers * bands * total,
        ),
    )(column_temp, depth)


def pool_kernel(grid_ref, rows_ref, cols_ref, out_ref):
    high = lax.Precision.HIGHEST
    kept = jnp.float32
    lines = jnp.dot(rows_ref[...], grid_ref[0], precision=high, preferred_element_type=kept)
    tiles = jnp.dot(lines, cols_ref[...], precision=high, preferred_element_type=kept)
    out_ref[0] = (tiles * 0.25).astype(jnp.bfloat16)


def halves(coarse, dtype):
    fine = jnp.arange(2 * coarse, dtype=jnp.int32) // 2
    return (jnp.arange(coarse, dtype=jnp.int32)[:, None] == fine[None, :]).astype(dtype)


def pool(grid):
    layers, lines, places = grid.shape
    rows, cols = lines // 2, places // 2
    return pl.pallas_call(
        pool_kernel,
        grid=(layers,),
        out_shape=jax.ShapeDtypeStruct((layers, rows, cols), jnp.bfloat16),
        in_specs=[
            pl.BlockSpec((1, lines, places), lambda l: (l, 0, 0)),
            pl.BlockSpec((rows, lines), lambda l: (0, 0)),
            pl.BlockSpec((places, cols), lambda l: (0, 0)),
        ],
        out_specs=pl.BlockSpec((1, rows, cols), lambda l: (l, 0, 0)),
        compiler_params=pltpu.CompilerParams(vmem_limit_bytes=24 << 20),
    )(grid, halves(rows, jnp.float32), halves(cols, jnp.float32).T)


def force_kernel(grid_ref, heat_ref, rows_ref, cols_ref, out_ref):
    wide = jnp.dot(heat_ref[0], cols_ref[...], preferred_element_type=jnp.float32)
    full = jnp.dot(
        rows_ref[...], wide.astype(jnp.bfloat16), preferred_element_type=jnp.float32
    )
    out_ref[0] = (grid_ref[0] + full).astype(jnp.bfloat16)


def force(grid, heat):
    layers, lines, places = grid.shape
    rows, cols = lines // 2, places // 2
    return pl.pallas_call(
        force_kernel,
        grid=(layers,),
        out_shape=jax.ShapeDtypeStruct((layers, lines, places), jnp.bfloat16),
        in_specs=[
            pl.BlockSpec((1, lines, places), lambda l: (l, 0, 0)),
            pl.BlockSpec((1, rows, cols), lambda l: (l, 0, 0)),
            pl.BlockSpec((lines, rows), lambda l: (0, 0)),
            pl.BlockSpec((cols, places), lambda l: (0, 0)),
        ],
        out_specs=pl.BlockSpec((1, lines, places), lambda l: (l, 0, 0)),
        compiler_params=pltpu.CompilerParams(vmem_limit_bytes=24 << 20),
    )(grid, heat, halves(rows, jnp.bfloat16).T, halves(cols, jnp.bfloat16))


def per_device(
    gaussian_thermal_state,
    radiation_holder_device,
    layer_opacity_depths,
    wavenumber_duos_placed,
    reduced_grid_sites,
    weighted_polynomial_basis,
):
    vertical_layer_pile, parallel_circle_lines, meridian_entries = gaussian_thermal_state.shape
    group = weighted_polynomial_basis.shape[0]
    nlat_all = weighted_polynomial_basis.shape[1]
    ndeg = weighted_polynomial_basis.shape[2]
    nwave = wavenumber_duos_placed.shape[0] * 2
    nlon = nwave * 2
    lat_size = lax.axis_size("lat")
    lon_size = lax.axis_size("lon")
    devices_all = lat_size * lon_size
    capacity = layer_opacity_depths.shape[3] // devices_all
    level_group = vertical_layer_pile // lon_size
    coarse_rows, coarse_cols = parallel_circle_lines // 2, meridian_entries // 2
    column_temp = pool(gaussian_thermal_state).reshape(
        vertical_layer_pile, coarse_rows * coarse_cols
    )
    owner = radiation_holder_device[0, :, 0]
    slots = owner * capacity + owner_ranks(owner, devices_all)
    outgoing = (
        jnp.zeros((vertical_layer_pile, devices_all * capacity), jnp.bfloat16)
        .at[:, slots]
        .set(column_temp)
    )
    arrived = lax.all_to_all(
        outgoing.reshape(vertical_layer_pile, devices_all, capacity),
        ("lat", "lon"),
        split_axis=1,
        concat_axis=1,
        tiled=True,
    )
    heating = radiate(
        arrived.reshape(vertical_layer_pile, devices_all * capacity), layer_opacity_depths[0]
    )
    returned = lax.all_to_all(
        heating.reshape(vertical_layer_pile, devices_all, capacity),
        ("lat", "lon"),
        split_axis=1,
        concat_axis=1,
        tiled=True,
    )
    column_heat = returned.reshape(vertical_layer_pile, devices_all * capacity)[:, slots].reshape(
        vertical_layer_pile, coarse_rows, coarse_cols
    )
    radiatively_driven_thermal = force(gaussian_thermal_state, column_heat)
    all_waves = wave_numbers(wavenumber_duos_placed, nwave)
    full_table = dft_table(all_waves, nlon)
    piece = lax.all_to_all(
        radiatively_driven_thermal, "lon", split_axis=0, concat_axis=2, tiled=True
    )
    points = level_group * parallel_circle_lines
    product = lax.dot_general(
        full_table,
        piece.reshape(points, nlon),
        (((0,), (1,)), ((), ())),
        preferred_element_type=jnp.float32,
    )
    keep_all = 2 * all_waves[:, None] < jnp.tile(reduced_grid_sites, level_group)[None, :]
    row_fourier = jnp.where(keep_all, product, 0.0).astype(jnp.bfloat16)
    gathered = lax.all_to_all(
        row_fourier.reshape(devices_all, 4 * group, points),
        ("lat", "lon"),
        split_axis=0,
        concat_axis=0,
        tiled=True,
    ).reshape(lat_size, lon_size, group, 4, level_group, parallel_circle_lines)
    fourier = gathered.transpose(2, 3, 1, 4, 0, 5).reshape(
        group, 4 * vertical_layer_pile, nlat_all
    )
    device_index = lax.axis_index("lat") * lon_size + lax.axis_index("lon")
    my_pairs = lax.dynamic_slice_in_dim(wavenumber_duos_placed, device_index * group, group)
    full = lax.dot_general(
        fourier,
        weighted_polynomial_basis,
        (((2,), (1,)), ((0,), (0,))),
        preferred_element_type=jnp.float32,
    )
    coeff = jnp.arange(ndeg, dtype=jnp.int32)[None, :]
    first = coeff < (nwave - my_pairs)[:, None]
    degree = jnp.where(first, my_pairs[:, None] + coeff, coeff - 1).astype(jnp.float32)
    factor = jnp.where(
        coeff <= nwave,
        1.0 / (1.0 + DIFFUSION * degree * (degree + 1.0) / (nwave * nwave)),
        0.0,
    )
    side = jnp.arange(4 * vertical_layer_pile, dtype=jnp.int32) < 2 * vertical_layer_pile
    chosen = first[:, None, :] == side[None, :, None]
    split = jnp.where(chosen, full * factor[:, None, :], 0.0).astype(jnp.bfloat16)
    synth = lax.dot_general(
        split,
        weighted_polynomial_basis,
        (((2,), (2,)), ((0,), (0,))),
        preferred_element_type=jnp.float32,
    ).astype(jnp.bfloat16)
    back = synth.reshape(
        group, 4, lon_size, level_group, lat_size, parallel_circle_lines
    ).transpose(4, 2, 0, 1, 3, 5)
    row_synth = lax.all_to_all(
        back.reshape(devices_all, 4 * group, points),
        ("lat", "lon"),
        split_axis=0,
        concat_axis=0,
        tiled=True,
    ).reshape(devices_all * 4 * group, points)
    lat_grid = lax.dot_general(
        row_synth, full_table, (((0,), (1,)), ((), ())), preferred_element_type=jnp.float32
    ).astype(jnp.bfloat16)
    lat_grid = lat_grid.reshape(level_group, parallel_circle_lines, nlon)
    tile = lax.all_to_all(lat_grid, "lon", split_axis=2, concat_axis=0, tiled=True)
    return tile.astype(jnp.float32)


def solution(mesh):
    in_specs = (
        P(None, "lat", "lon"),
        P(("lat", "lon"), None, None),
        P(("lat", "lon"), None, None, None),
        P(),
        P("lat"),
        P(("lat", "lon"), None, None),
    )
    out_specs = P(None, "lat", "lon")
    return jax.shard_map(
        per_device, mesh=mesh, in_specs=in_specs, out_specs=out_specs, check_vma=False
    )
```
